32 devices in a mesh: groups: 1, ctx: 16 (over z, y, x), exp: 2 (over core).
Axes of the slice: x: 2, y: 2, z: 4, core: 2. Of those that a mesh axis runs over, the one named last changes fastest.
Arguments:
- queries: bfloat16 [2048, 2048], P(('groups', 'ctx'), 'exp'), may hold values from -40 to 40
- key_rows: bfloat16 [2048, 256], P(('groups', 'ctx'), 'exp'), may hold values from -15 to 15
- value_rows: bfloat16 [2048, 256], P(('groups', 'ctx'), 'exp'), may hold values from -6 to 6
- hidden_in: bfloat16 [2048, 1024], P(('groups', 'ctx')), may hold values from -40 to 40
- out_proj: bfloat16 [2048, 1024], P('exp'), may hold values from -0.125 to 0.125
- norm_gain: float32 [1024], replicated, may hold values from 0.1 to 1.9
- expert_ids: int32 [2048, 8], P(('groups', 'ctx')), may hold values from 0 to 15, all different within a row; in each aligned block of 128 rows (0 to 127, 128 to 255, ...) at most 96 rows name the same one
- gate_scores: float32 [2048, 8], P(('groups', 'ctx')), may hold values from 0.05 to 1
- w_gate: bfloat16 [16, 1024, 384], P('ctx'), may hold values from -0.1875 to 0.1875
- w_up: bfloat16 [16, 1024, 384], P('ctx'), may hold values from -0.1875 to 0.1875
- w_down: bfloat16 [16, 384, 1024], P('ctx'), may hold values from -0.3125 to 0.3125
Outputs:
- layer_out: bfloat16 [2048, 1024], P(('groups', 'ctx'), 'exp')
The draws below stay inside these ranges and needn't reach their ends.
Inputs may be any that keep to these rules, and one draw needn't show every extreme that they name: `expert_ids`: each row names 8 different experts. No expert is named by more than 96 rows of one aligned block of 128 rows, a bound that some block reaches.
All inputs are finite; a program needn't handle non-finite values.
Results may differ from the reference program's by a relative error of at most 0.0035.
Values may be sent and summed in bfloat16 or wider, within the bound.
A program may use at most 64 MiB of HBM per device.

```python
import math
import jax
import jax.numpy as jnp
import numpy as np
from jax import lax

D = 1024
HQ = 16
HK = 2
HD = 128
FF = 384
TOPK = 8
TOK_DEV = 128
S = 2048
EXPERTS = 16
CAP = 96
N_CTX = 16


def query_key_pair(key):
    parts = jax.random.split(jax.random.fold_in(key, 23), 2)
    query_all = 3.0 * jax.random.normal(parts[0], (S, HQ * HD), jnp.float32)
    key_all = jax.random.normal(parts[1], (S, HK * HD), jnp.float32)
    return (jnp.clip(query_all, -40.0, 40.0), jnp.clip(key_all, -15.0, 15.0))


def draw_queries(key, part):
    return query_key_pair(key)[0].astype(jnp.bfloat16)


def draw_key_rows(key, part):
    return query_key_pair(key)[1].astype(jnp.bfloat16)


def draw_hidden_in(key, part):
    parts = jax.random.split(jax.random.fold_in(key, 7), 3)
    row_scale = jnp.exp(jax.random.uniform(parts[0], (S, 1), jnp.float32, math.log(0.3), math.log(3.0)))
    ramp = jnp.exp(jnp.linspace(0.0, math.log(3.0), D)).astype(jnp.float32)
    col_scale = ramp[None, :] * jnp.exp(jax.random.uniform(parts[1], (1, D), jnp.float32, 0.0, math.log(3.0)))
    base = jax.random.normal(parts[2], (S, D), jnp.float32)
    return jnp.clip(base * row_scale * col_scale, -40.0, 40.0).astype(jnp.bfloat16)


def shard_levels(key, extent, cuts, smallest, largest):
    def one(position, blocks):
        draws = jax.random.uniform(jax.random.fold_in(jax.random.fold_in(key, 6), position), (blocks,), jnp.float32, smallest / len(cuts), largest / len(cuts))
        return jnp.repeat(jnp.exp(draws), extent[position] // blocks).reshape((-1,) + (1,) * (len(extent) - position - 1))

    level = one(*cuts[0])
    for cut in cuts[1:]:
        level = level * one(*cut)
    return level


def routed_block(own_key, own, number, rows, number_of, top, bound, slope):
    ranking = jax.random.permutation(own_key, number_of)
    heavy_load, usual = portions_of(number_of, rows * top, bound, slope, True), portions_of(number_of, rows * top, bound, slope, False)
    places = jnp.arange(number_of)

    def named(sizes, turn):
        used = int((sizes > 0).sum())
        fixed = max(1, used // 4)
        shifted = fixed + (places - fixed + turn * (used - fixed)) % max(1, number_of - fixed)
        return jnp.zeros((number_of,), jnp.int32).at[ranking[jnp.where(places < fixed, places, shifted)]].set(jnp.asarray(sizes, jnp.int32))

    sizes = jnp.where(number % 4 == 0, named(heavy_load, number // 4), named(usual, number - number // 4 - 1))
    mixed = jax.random.permutation(jax.random.fold_in(own, 3), number_of)
    donor, sink = mixed[0:number_of // 2 * 2:2], mixed[1:number_of // 2 * 2:2]
    margin = jnp.minimum(sizes[donor] - 1, bound - sizes[sink]) // 2
    margin = jnp.where((donor == ranking[0]) | (sink == ranking[0]) | (sizes[sink] == 0), 0, jnp.maximum(margin, 0))
    shifted = jax.random.randint(jax.random.fold_in(own, 4), (number_of // 2,), 0, 1 << 20) % (margin + 1)
    sizes = sizes.at[donor].add(-shifted).at[sink].add(shifted)
    labels = jnp.searchsorted(jnp.cumsum(sizes), jnp.arange(rows * top), side="right").astype(jnp.int32)
    grid = labels.reshape(top, rows).T
    grid = grid[jax.random.permutation(jax.random.fold_in(own, 1), rows)]
    turn = jax.random.randint(jax.random.fold_in(own, 2), (rows, 1), 0, top)
    return jnp.take_along_axis(grid, (jnp.arange(top)[None, :] + turn) % top, axis=1)


def portions_of(count, total, bound, skew, full):
    portions = [(1 << 20) // math.isqrt(rank ** skew) + 1 for rank in range(1, count + 1)]
    largest = bound if full else min(bound, max(-(-total // count), total * portions[0] // sum(portions)))
    least = 1 if total - largest >= count - 1 else 0
    holding, spare = [largest] + [least] * (count - 1), total - largest - least * (count - 1)
    while spare > 0:
        movable = [i for i in range(1, count) if holding[i] < largest] or [i for i in range(1, count) if holding[i] < bound]
        mass, budget = sum([portions[i] for i in movable]), spare
        for i in movable:
            addition = min(bound - holding[i], max(1, budget * portions[i] // mass), spare)
            holding[i] = holding[i] + addition
            spare = spare - addition
    return np.array(holding)


def scatter_about(own_key, extent, scale, limit, cuts=(), held_as=jnp.bfloat16):
    values = scale * jax.random.normal(own_key, extent, jnp.float32)
    if cuts:
        values = values * shard_levels(own_key, extent, cuts, -0.22, 0.18)
    return jnp.clip(values, -limit, limit).astype(held_as)


def setup_inputs(seed: int = 0, part: int = 0) -> dict:
    key_of = jax.random.split(jax.random.key(seed), 12)
    own_keys = jax.random.split(jax.random.fold_in(key_of[11], part), 12)
    queries = draw_queries(jax.random.fold_in(jax.random.fold_in(key_of[11], part), 71), part)
    key_rows = draw_key_rows(jax.random.fold_in(jax.random.fold_in(key_of[11], part), 71), part)
    value_rows = scatter_about(own_keys[2], (S, HK * HD), 1.0, 6.0, ((0, 16), (1, 2)))
    hidden_in = draw_hidden_in(jax.random.fold_in(jax.random.fold_in(key_of[11], part), 71), part)
    out_proj = scatter_about(key_of[4], (HQ * HD, D), (HQ * HD) ** -0.5, 0.125, ((0, 2),))
    norm_gain = jnp.clip(1.0 + 0.18 * jax.random.normal(key_of[5], (D,), jnp.float32), 0.1, 1.9)
    expert_ids_keys = jax.random.split(jax.random.fold_in(own_keys[6], 1), S // TOK_DEV)
    expert_ids_turns = jax.random.permutation(jax.random.fold_in(own_keys[6], 3), S // TOK_DEV)
    expert_ids = jax.vmap(lambda own, number: routed_block(jax.random.fold_in(own_keys[6], 2), own, number, TOK_DEV, EXPERTS, TOPK, CAP, 2))(expert_ids_keys, expert_ids_turns).reshape((S, TOPK))
    gate_scores = jnp.clip(0.05 + 0.95 * jax.random.uniform(own_keys[7], (S, TOPK), jnp.float32) ** shard_levels(own_keys[7], (S, TOPK), ((0, 16),), -0.2, 0.2), 0.05, 1.0)
    w_gate = scatter_about(key_of[8], (EXPERTS, D, FF), D ** -0.5, 0.1875, ((0, 16),))
    w_up = scatter_about(key_of[9], (EXPERTS, D, FF), D ** -0.5, 0.1875, ((0, 16),))
    w_down = scatter_about(key_of[10], (EXPERTS, FF, D), FF ** -0.5, 0.3125, ((0, 16),))
    return dict(queries=queries, key_rows=key_rows, value_rows=value_rows, hidden_in=hidden_in, out_proj=out_proj, norm_gain=norm_gain, expert_ids=expert_ids, gate_scores=gate_scores, w_gate=w_gate, w_up=w_up, w_down=w_down)


def attention(queries, key_rows, value_rows):
    group = HQ // HK
    width = math.gcd(S, 128)
    key_all = key_rows.astype(jnp.float32).reshape(S, HK, HD)
    value_all = value_rows.astype(jnp.float32).reshape(S, HK, HD)
    key_pos = jnp.arange(S, dtype=jnp.int32)

    def one_block(start):
        block = lax.dynamic_slice_in_dim(queries, start, width, 0).astype(jnp.float32)
        block = block.reshape(width, HK, group, HD)
        scores = jnp.einsum('bkgd,tkd->kgbt', block, key_all) * HD ** (-0.5)
        query_pos = start + jnp.arange(width, dtype=jnp.int32)
        allowed = key_pos[None, :] <= query_pos[:, None]
        scores = jnp.where(allowed, scores, -jnp.inf)
        peak = lax.optimization_barrier(jnp.max(scores, axis=-1, keepdims=True))
        weights = jnp.exp(scores - peak)
        total = lax.optimization_barrier(jnp.sum(weights, axis=-1))
        rounded = weights.astype(jnp.bfloat16).astype(jnp.float32)
        summed = jnp.einsum('kgbt,tkd->kgbd', rounded, value_all)
        output = summed / total[..., None]
        output = jnp.transpose(output, (2, 0, 1, 3)).reshape(width, HQ * HD)
        return output.astype(jnp.bfloat16)
    starts = jnp.arange(S // width, dtype=jnp.int32) * width
    return lax.map(one_block, starts).reshape(S, HQ * HD)

def experts_out(normed, expert_ids, gate_scores, w_gate, w_up, w_down):
    slots = S * TOPK
    flat_ids = expert_ids.reshape(slots).astype(jnp.int32)
    flat_token = jnp.arange(slots, dtype=jnp.int32) // TOPK
    mixing = (gate_scores / lax.optimization_barrier(jnp.sum(gate_scores, axis=1, keepdims=True))).reshape(slots)
    order = jnp.argsort(flat_ids, stable=True).astype(jnp.int32)
    sorted_token = flat_token[order]
    sorted_weight = mixing[order]
    counts = lax.optimization_barrier(jnp.sum((flat_ids[:, None] == jnp.arange(EXPERTS, dtype=jnp.int32)[None, :]).astype(jnp.int32), axis=0))
    starts = (jnp.cumsum(counts) - counts).astype(jnp.int32)
    most = N_CTX * CAP

    def one_expert(total, inputs):
        gate_mat, up_mat, down_mat, start, count = inputs
        offsets = jnp.arange(most, dtype=jnp.int32)
        index = jnp.minimum(start + offsets, slots - 1).astype(jnp.int32)
        live = offsets < count
        row_token = sorted_token[index]
        rows = normed[row_token]
        gate = jnp.dot(rows, gate_mat, preferred_element_type=jnp.float32)
        upper = jnp.dot(rows, up_mat, preferred_element_type=jnp.float32)
        hidden = (jax.nn.silu(gate) * upper).astype(jnp.bfloat16)
        part = jnp.dot(hidden, down_mat, preferred_element_type=jnp.float32).astype(jnp.bfloat16)
        factor = jnp.where(live, sorted_weight[index], jnp.zeros_like(sorted_weight[index]))
        contrib = part.astype(jnp.float32) * factor[:, None]
        return (total.at[row_token].add(contrib), None)
    start_total = jnp.zeros((S, D), jnp.float32)
    total, _ = lax.scan(one_expert, start_total, (w_gate, w_up, w_down, starts, counts))
    return total

def reference(queries, key_rows, value_rows, hidden_in, out_proj, norm_gain, expert_ids, gate_scores, w_gate, w_up, w_down):
    attended = attention(queries, key_rows, value_rows)
    resid = hidden_in.astype(jnp.float32) + jnp.dot(attended, out_proj, preferred_element_type=jnp.float32)
    inverse = lax.rsqrt(lax.optimization_barrier(jnp.mean(resid * resid, axis=1, keepdims=True)) + 1e-06)
    normed = (resid * inverse * norm_gain.astype(jnp.float32)[None, :]).astype(jnp.bfloat16)
    expert_sum = experts_out(normed, expert_ids, gate_scores, w_gate, w_up, w_down)
    return (resid + expert_sum).astype(jnp.bfloat16)
```

```python
import functools
import math

import jax
import jax.numpy as jnp
from jax import lax
from jax.experimental import pallas as pl
from jax.experimental.pallas import tpu as pltpu
from jax.sharding import PartitionSpec as P

MESH = pl.DeviceIdType.MESH
HEAD = 128
PIECES = 2
NEG = -1e30
STAGGER = 1


def attend(queries, key_rows, value_rows, first):
    token_count = queries.shape[0]
    kv_heads = key_rows.shape[1] // 128
    q_heads = queries.shape[1] // 128
    group = q_heads // kv_heads
    grouped = queries.reshape(token_count, kv_heads, group, 128)
    query_pos = first + jnp.arange(token_count, dtype=jnp.int32)
    last_pos = first + token_count - 1
    scale = 128 ** (-0.5)
    shape_rows = (kv_heads, group, token_count)
    start_state = (
        jnp.full(shape_rows, -1e30, jnp.float32),
        jnp.zeros(shape_rows, jnp.float32),
        jnp.zeros(shape_rows + (128,), jnp.float32),
    )
    key_piece = lax.all_gather(key_rows, "ctx", axis=0, tiled=True)
    value_piece = lax.all_gather(value_rows, "ctx", axis=0, tiled=True)
    count = key_piece.shape[0]
    width = math.gcd(count, 512)

    def step(block_index, state):
        offset = block_index * width

        def compute(inner):
            running_max, running_sum, accum = inner
            key_block = lax.dynamic_slice_in_dim(key_piece, block_index * width, width, 0).reshape(
                width, kv_heads, 128
            )
            value_block = lax.dynamic_slice_in_dim(
                value_piece, block_index * width, width, 0
            ).reshape(width, kv_heads, 128)
            scores = (
                jnp.einsum("tkgd,skd->kgts", grouped, key_block, preferred_element_type=jnp.float32)
                * scale
            )
            key_pos = offset + jnp.arange(width, dtype=jnp.int32)
            allowed = key_pos[None, :] <= query_pos[:, None]
            scores = jnp.where(allowed, scores, -jnp.inf)
            new_max = jnp.maximum(running_max, jnp.max(scores, axis=-1))
            factor = jnp.exp(running_max - new_max)
            weights = jnp.exp(scores - new_max[..., None])
            new_sum = running_sum * factor + jnp.sum(weights, axis=-1)
            product = jnp.einsum(
                "kgts,skd->kgtd",
                weights.astype(jnp.bfloat16),
                value_block,
                preferred_element_type=jnp.float32,
            )
            return (new_max, new_sum, accum * factor[..., None] + product)

        return lax.cond(offset <= last_pos, compute, lambda inner: inner, state)

    _, total, accum = lax.fori_loop(0, count // width, step, start_state)
    output = accum / total[..., None]
    return (
        jnp.transpose(output, (2, 0, 1, 3)).reshape(token_count, q_heads * 128).astype(jnp.bfloat16)
    )


def place_rows(expert_ids, sent_rows, capacity, expert_count):
    top_count = expert_ids.shape[1]
    flat_ids = expert_ids.reshape(-1)
    onehot = (flat_ids[:, None] == jnp.arange(expert_count, dtype=jnp.int32)[None, :]).astype(
        jnp.int32
    )
    index = jnp.arange(flat_ids.shape[0], dtype=jnp.int32)
    before = (index[None, :] < index[:, None]).astype(jnp.bfloat16)
    earlier = jnp.dot(
        before, onehot.astype(jnp.bfloat16), preferred_element_type=jnp.float32
    ).astype(jnp.int32)
    slot_index = jnp.sum(earlier * onehot, axis=1)
    destination = flat_ids * capacity + slot_index
    copies = jnp.repeat(sent_rows, top_count, axis=0)
    buffer = (
        jnp.zeros((expert_count * capacity, sent_rows.shape[1]), sent_rows.dtype)
        .at[destination]
        .set(copies)
    )
    return (buffer.reshape(expert_count, 2, capacity // 2, sent_rows.shape[1]), destination)


def per_device(
    queries,
    key_rows,
    value_rows,
    hidden_in,
    out_proj,
    norm_gain,
    expert_ids,
    gate_scores,
    w_gate,
    w_up,
    w_down,
):
    token_count = queries.shape[0]
    model_width = hidden_in.shape[1]
    half_width = model_width // 2
    ctx_size = lax.axis_size("ctx")
    local_experts = w_gate.shape[0]
    expert_count = local_experts * ctx_size
    top_count = expert_ids.shape[1]
    capacity = 2 * (
        min(token_count, max(2, 3 * token_count * top_count // (2 * expert_count))) // 2
    )
    half_cap = capacity // 2
    first = lax.axis_index("ctx") * token_count
    core = lax.axis_index("exp")
    side_start = core * half_width
    attended = attend(queries, key_rows, value_rows, first)
    head_part = jnp.dot(attended, out_proj, preferred_element_type=jnp.float32)
    attn_full = lax.psum(head_part.astype(jnp.bfloat16), "exp").astype(jnp.float32)
    resid = hidden_in.astype(jnp.float32) + attn_full
    inverse = lax.rsqrt(jnp.mean(resid * resid, axis=1, keepdims=True) + 1e-06)
    sent_rows = (resid * inverse * norm_gain[None, :]).astype(jnp.bfloat16)
    resid_half = lax.dynamic_slice_in_dim(resid, side_start, half_width, 1)
    buffer, destination = place_rows(expert_ids, sent_rows, capacity, expert_count)
    own_slots = lax.dynamic_slice_in_dim(buffer, core, 1, 1)
    grouped = lax.all_to_all(own_slots, "ctx", split_axis=0, concat_axis=0, tiled=True)
    gate = jnp.einsum("sxmd,xdf->sxmf", grouped, w_gate, preferred_element_type=jnp.float32)
    upper = jnp.einsum("sxmd,xdf->sxmf", grouped, w_up, preferred_element_type=jnp.float32)
    hidden = (jax.nn.silu(gate) * upper).astype(jnp.bfloat16)
    partial_value = jnp.einsum(
        "sxmf,xfd->sxmd", hidden, w_down, preferred_element_type=jnp.float32
    ).astype(jnp.bfloat16)
    returned = lax.all_to_all(partial_value, "ctx", split_axis=0, concat_axis=0, tiled=True)
    flat_back = returned.reshape(expert_count * half_cap, model_width)
    slot_of = destination % capacity
    expert_of = destination // capacity
    owned = slot_of // half_cap == core
    local_index = jnp.where(owned, expert_of * half_cap + slot_of - core * half_cap, 0)
    picked = flat_back[local_index].astype(jnp.float32)
    mixing = (gate_scores / jnp.sum(gate_scores, axis=1, keepdims=True)).reshape(-1)
    mixing = jnp.where(owned, mixing, 0.0)
    weighted = (picked * mixing[:, None]).reshape(token_count, top_count, model_width)
    mixed_part = jnp.sum(weighted, axis=1)
    moe_half = lax.psum_scatter(
        mixed_part.astype(jnp.bfloat16), "exp", scatter_dimension=1, tiled=True
    ).astype(jnp.float32)
    return (resid_half + moe_half).astype(jnp.bfloat16)


def layer_kernel(
    n,
    q_ref,
    k_ref,
    v_ref,
    hid_ref,
    proj_hbm,
    gain_ref,
    ids_ref,
    gate_ref,
    wg_hbm,
    wu_hbm,
    wd_hbm,
    out_ref,
    kv_buf,
    co_buf,
    row_buf,
    con_buf,
    rs_bufs,
    half_out,
    half_in,
    fin_out,
    fin_in,
    queries,
    top,
    den,
    acc,
    att,
    resid,
    by_token,
    proj,
    wg,
    wu,
    wd,
    load_sem,
    kv_sem,
    co_sem,
    ag_sem,
    rs_sem,
    half_sem,
    fin_sem,
):
    me = lax.axis_index("ctx")
    core = lax.axis_index("exp")
    group = lax.axis_index("groups")
    bits = n.bit_length() - 1
    rows = q_ref.shape[0]
    heads = q_ref.shape[1] // HEAD
    half = rows // 2
    piece_rows = half // PIECES
    width = hid_ref.shape[1]
    side = width // 2
    coord = [(me // 2 ** (bits - 1 - d)) % 2 for d in range(bits)]
    partner = [me + (1 - 2 * coord[d]) * 2 ** (bits - 1 - d) for d in range(bits)]
    forward = list(range(bits))
    crossed = forward[:-2] + [forward[-1], forward[-2]]
    orders = [forward if p % 2 == 0 else crossed for p in range(PIECES)]
    other = 1 - core

    loads = [
        pltpu.make_async_copy(src, dst, load_sem.at[i])
        for i, (src, dst) in enumerate(
            [(proj_hbm, proj), (wg_hbm.at[0], wg), (wu_hbm.at[0], wu), (wd_hbm.at[0], wd)]
        )
    ]
    for load in loads:
        load.start()

    barrier = pltpu.get_barrier_semaphore()
    for d in range(bits):
        pl.semaphore_signal(
            barrier, inc=1, device_id=(group, partner[d], core), device_id_type=MESH
        )
    pl.semaphore_signal(barrier, inc=1, device_id=(group, me, other), device_id_type=MESH)

    own = tuple(coord)
    kv_buf[(0,) + own] = k_ref[...]
    kv_buf[(1,) + own] = v_ref[...]
    mix = gate_ref[...] / jnp.sum(gate_ref[...], axis=1, keepdims=True)
    lane = lax.broadcasted_iota(jnp.int32, (rows, HEAD), 1)
    coef = jnp.zeros((rows, HEAD), jnp.float32)
    for k in range(ids_ref.shape[1]):
        coef = coef + jnp.where(ids_ref[:, k : k + 1] == lane, mix[:, k : k + 1], 0.0)
    co_buf[own] = coef.T[: co_buf.shape[bits]]
    pl.semaphore_wait(barrier, bits + 1)

    def gather(buf, lead, order, step, sems):
        done = order[:step]
        where = lead + tuple(slice(None) if d in done else coord[d] for d in range(bits))
        return pltpu.make_async_remote_copy(
            src_ref=buf.at[where],
            dst_ref=buf.at[where],
            send_sem=sems[0],
            recv_sem=sems[1],
            device_id=(group, partner[order[step]], core),
            device_id_type=MESH,
        )

    sent = []

    def kv_copies(step):
        copies = [
            gather(
                kv_buf,
                (i,),
                [forward, crossed][i],
                step,
                (kv_sem.at[i, step, 0], kv_sem.at[i, step, 1]),
            )
            for i in range(2)
        ]
        copies.append(
            gather(co_buf, (), forward, step, (co_sem.at[step, 0], co_sem.at[step, 1]))
        )
        return copies

    for step in range(bits):
        copies = kv_copies(step)
        for copy in copies:
            copy.start()
        if step == 0:
            for h in range(heads):
                queries[h] = q_ref[:, h * HEAD : (h + 1) * HEAD]
            top[...] = jnp.full(top.shape, NEG, jnp.float32)
            den[...] = jnp.zeros(den.shape, jnp.float32)
            acc[...] = jnp.zeros(acc.shape, jnp.float32)
        for copy in copies:
            copy.wait_recv()
        sent += copies

    span = 4 * rows
    chunk = me // 4
    unit = HEAD ** (-0.5) * math.log2(math.e)
    row_pos = lax.broadcasted_iota(jnp.int32, (rows, span), 0) + (me % 4) * rows
    col_pos = lax.broadcasted_iota(jnp.int32, (rows, span), 1)

    def attend_chunk(j, carry):
        at = tuple((j // 2 ** (bits - 3 - d)) % 2 for d in range(bits - 2))
        keys = kv_buf[(0,) + at].reshape(span, HEAD)
        values = kv_buf[(1,) + at].reshape(span, HEAD)
        allowed = col_pos <= row_pos + (chunk - j) * span
        for h in range(heads):
            scores = lax.dot_general(
                queries[h], keys, (((1,), (1,)), ((), ())), preferred_element_type=jnp.float32
            )
            scores = jnp.where(allowed, scores, NEG)
            old = top[h][:, :1]
            new = jnp.maximum(old, jnp.max(scores, axis=1, keepdims=True))
            factor = jnp.exp2((old - new) * unit)
            weights = jnp.exp2((scores - new) * unit)
            total = den[h][:, :1] * factor + jnp.sum(weights, axis=1, keepdims=True)
            product = jnp.dot(
                weights.astype(jnp.bfloat16), values, preferred_element_type=jnp.float32
            )
            acc[h] = acc[h] * factor + product
            top[h] = jnp.broadcast_to(new, (rows, HEAD))
            den[h] = jnp.broadcast_to(total, (rows, HEAD))
        return carry

    lax.fori_loop(0, chunk + 1, attend_chunk, 0)
    for h in range(heads):
        att[:, h * HEAD : (h + 1) * HEAD] = (acc[h] / den[h]).astype(jnp.bfloat16)

    loads[0].wait()
    mine = pl.ds(pl.multiple_of(core * half, half), half)
    theirs = pl.ds(pl.multiple_of(other * half, half), half)
    half_out[...] = jnp.dot(
        att[theirs, :], proj[...], preferred_element_type=jnp.float32
    ).astype(jnp.bfloat16)
    swap = pltpu.make_async_remote_copy(
        src_ref=half_out,
        dst_ref=half_in,
        send_sem=half_sem.at[0],
        recv_sem=half_sem.at[1],
        device_id=(group, me, other),
        device_id_type=MESH,
    )
    swap.start()
    resid[...] = hid_ref[mine, :].astype(jnp.float32) + jnp.dot(
        att[mine, :], proj[...], preferred_element_type=jnp.float32
    )
    by_token[...] = jnp.zeros(by_token.shape, jnp.float32)
    for b in range(n):
        at = tuple((b // 2 ** (bits - 1 - d)) % 2 for d in range(bits))
        by_token[b : b + 1, :] = co_buf[at + (pl.ds(me, 1), slice(None))]
    by_token[...] = by_token[...].T
    swap.wait_recv()
    sent.append(swap)
    full = resid[...] + half_in[...].astype(jnp.float32)
    resid[...] = full
    inverse = lax.rsqrt(jnp.mean(full * full, axis=1, keepdims=True) + 1e-06)
    normed = (full * inverse * gain_ref[...]).astype(jnp.bfloat16)

    def row_copy(p, step):
        return gather(
            row_buf, (p,), orders[p], step, (ag_sem.at[p, step, 0], ag_sem.at[p, step, 1])
        )

    def rs_copy(p, step):
        order = orders[p][::-1]
        done = order[:step]
        turn = order[step]
        where = (p,) + tuple(
            coord[d] if d in done else (1 - coord[d] if d == turn else slice(None))
            for d in range(bits)
        )
        return pltpu.make_async_remote_copy(
            src_ref=con_buf.at[where],
            dst_ref=rs_bufs[step].at[p],
            send_sem=rs_sem.at[p, step, 0],
            recv_sem=rs_sem.at[p, step, 1],
            device_id=(group, partner[turn], core),
            device_id_type=MESH,
        )

    def fin_copy(p):
        return pltpu.make_async_remote_copy(
            src_ref=fin_out.at[p],
            dst_ref=fin_in.at[p],
            send_sem=fin_sem.at[p, 0],
            recv_sem=fin_sem.at[p, 1],
            device_id=(group, me, other),
            device_id_type=MESH,
        )

    def experts(p):
        if p == 0:
            for load in loads[1:]:
                load.wait()
        count = n * piece_rows
        x = row_buf[p].reshape(count, width)
        gate = jnp.dot(x, wg[...], preferred_element_type=jnp.float32)
        upper = jnp.dot(x, wu[...], preferred_element_type=jnp.float32)
        hidden = (gate / (1.0 + jnp.exp(-gate)) * upper).astype(jnp.bfloat16)
        part = jnp.dot(hidden, wd[...], preferred_element_type=jnp.float32)
        first = pl.multiple_of(core * half + p * piece_rows, piece_rows)
        columns = by_token[pl.ds(first, piece_rows), :]
        for b in range(n):
            at = tuple((b // 2 ** (bits - 1 - d)) % 2 for d in range(bits))
            con_buf[(p,) + at] = (
                part[b * piece_rows : (b + 1) * piece_rows] * columns[:, b : b + 1]
            ).astype(jnp.bfloat16)

    def stage(p, s):
        if s == 0:
            row_buf[(p,) + own] = normed[p * piece_rows : (p + 1) * piece_rows]
            row_copy(p, 0).start()
            return
        if s <= bits:
            copy = row_copy(p, s - 1)
            copy.wait_recv()
            sent.append(copy)
            if s < bits:
                row_copy(p, s).start()
                return
            experts(p)
            rs_copy(p, 0).start()
            return
        s -= bits + 1
        if s < bits:
            copy = rs_copy(p, s)
            copy.wait_recv()
            sent.append(copy)
            order = orders[p][::-1]
            where = (p,) + tuple(
                coord[d] if d in order[: s + 1] else slice(None) for d in range(bits)
            )
            total = con_buf[where].astype(jnp.float32) + rs_bufs[s][p].astype(jnp.float32)
            if s < bits - 1:
                con_buf[where] = total.astype(jnp.bfloat16)
                rs_copy(p, s + 1).start()
                return
            result = resid[p * piece_rows : (p + 1) * piece_rows] + total
            result = result.astype(jnp.bfloat16)
            left, right = result[:, :side], result[:, side:]
            fin_out[p] = jnp.where(core == 0, right, left)
            fin_copy(p).start()
            first = pl.multiple_of(core * half + p * piece_rows, piece_rows)
            out_ref[pl.ds(first, piece_rows), :] = jnp.where(core == 0, left, right)
            return
        copy = fin_copy(p)
        copy.wait_recv()
        sent.append(copy)
        first = pl.multiple_of(other * half + p * piece_rows, piece_rows)
        out_ref[pl.ds(first, piece_rows), :] = fin_in[p]

    stages = 2 * bits + 2
    plan = sorted((s + STAGGER * p, p, s) for p in range(PIECES) for s in range(stages))
    for _, p, s in plan:
        stage(p, s)
    for copy in sent:
        copy.wait_send()


def fused_layer(n, *args):
    queries, key_rows, value_rows, hidden_in, out_proj = args[:5]
    norm_gain, expert_ids, gate_scores, w_gate, w_up, w_down = args[5:]
    rows, width = hidden_in.shape
    heads = queries.shape[1] // HEAD
    bits = n.bit_length() - 1
    half = rows // 2
    piece_rows = half // PIECES
    cube = (2,) * bits
    vmem = pl.BlockSpec(memory_space=pltpu.VMEM)
    anywhere = pl.BlockSpec(memory_space=pl.ANY)
    bf16, f32 = jnp.bfloat16, jnp.float32
    scratch = [
        pltpu.VMEM((2,) + cube + (rows, HEAD), bf16),
        pltpu.VMEM(cube + (-(-n // 8) * 8, rows), f32),
        pltpu.VMEM((PIECES,) + cube + (piece_rows, width), bf16),
        pltpu.VMEM((PIECES,) + cube + (piece_rows, width), bf16),
        [
            pltpu.VMEM((PIECES,) + cube[s + 1 :] + (piece_rows, width), bf16)
            for s in range(bits)
        ],
        pltpu.VMEM((half, width), bf16),
        pltpu.VMEM((half, width), bf16),
        pltpu.VMEM((PIECES, piece_rows, width // 2), bf16),
        pltpu.VMEM((PIECES, piece_rows, width // 2), bf16),
        pltpu.VMEM((heads, rows, HEAD), bf16),
        pltpu.VMEM((heads, rows, HEAD), f32),
        pltpu.VMEM((heads, rows, HEAD), f32),
        pltpu.VMEM((heads, rows, HEAD), f32),
        pltpu.VMEM((rows, heads * HEAD), bf16),
        pltpu.VMEM((half, width), f32),
        pltpu.VMEM((rows, rows), f32),
        pltpu.VMEM(out_proj.shape, bf16),
        pltpu.VMEM(w_gate.shape[1:], bf16),
        pltpu.VMEM(w_up.shape[1:], bf16),
        pltpu.VMEM(w_down.shape[1:], bf16),
        pltpu.SemaphoreType.DMA((4,)),
        pltpu.SemaphoreType.DMA((2, bits, 2)),
        pltpu.SemaphoreType.DMA((bits, 2)),
        pltpu.SemaphoreType.DMA((PIECES, bits, 2)),
        pltpu.SemaphoreType.DMA((PIECES, bits, 2)),
        pltpu.SemaphoreType.DMA((2,)),
        pltpu.SemaphoreType.DMA((PIECES, 2)),
    ]
    return pl.pallas_call(
        functools.partial(layer_kernel, n),
        out_shape=jax.ShapeDtypeStruct((rows, width // 2), bf16),
        in_specs=[vmem] * 4 + [anywhere] + [vmem] * 3 + [anywhere] * 3,
        out_specs=vmem,
        scratch_shapes=scratch,
        compiler_params=pltpu.CompilerParams(
            collective_id=0, has_side_effects=True, vmem_limit_bytes=48 * 2**20
        ),
    )(
        queries,
        key_rows,
        value_rows,
        hidden_in,
        out_proj,
        norm_gain.reshape(1, width),
        expert_ids,
        gate_scores,
        w_gate,
        w_up,
        w_down,
    )


def fits_fused(n, cores, args):
    queries, key_rows, hidden_in = args[0], args[1], args[3]
    expert_ids, w_gate = args[6], args[8]
    rows, width = hidden_in.shape
    return (
        cores == 2
        and n >= 8
        and n & (n - 1) == 0
        and n <= HEAD
        and w_gate.shape[0] == 1
        and 2 * expert_ids.shape[1] >= n
        and key_rows.shape[1] == HEAD
        and rows == HEAD
        and width % (2 * HEAD) == 0
        and n * rows * width * 2 <= 8 * 2**20
    )


def layer(*args):
    n, cores = lax.axis_size("ctx"), lax.axis_size("exp")
    if fits_fused(n, cores, args):
        return fused_layer(n, *args)
    return per_device(*args)


def solution(mesh):
    placed = (
        P(("groups", "ctx"), "exp"),
        P(("groups", "ctx"), "exp"),
        P(("groups", "ctx"), "exp"),
        P(("groups", "ctx"), None),
        P("exp", None),
        P(),
        P(("groups", "ctx"), None),
        P(("groups", "ctx"), None),
        P("ctx", None, None),
        P("ctx", None, None),
        P("ctx", None, None),
    )
    return jax.shard_map(
        layer,
        mesh=mesh,
        in_specs=placed,
        out_specs=P(("groups", "ctx"), "exp"),
        check_vma=False,
    )
```

```python
import functools
import math

import jax
import jax.numpy as jnp
from jax import lax
from jax.experimental import pallas as pl
from jax.experimental.pallas import tpu as pltpu
from jax.sharding import PartitionSpec as P

MESH = pl.DeviceIdType.MESH
HEAD = 128
PIECES = 4
NEG = -1e30
STAGGER = 0


def attend(queries, key_rows, value_rows, first):
    token_count = queries.shape[0]
    kv_heads = key_rows.shape[1] // 128
    q_heads = queries.shape[1] // 128
    group = q_heads // kv_heads
    grouped = queries.reshape(token_count, kv_heads, group, 128)
    query_pos = first + jnp.arange(token_count, dtype=jnp.int32)
    last_pos = first + token_count - 1
    scale = 128 ** (-0.5)
    shape_rows = (kv_heads, group, token_count)
    start_state = (
        jnp.full(shape_rows, -1e30, jnp.float32),
        jnp.zeros(shape_rows, jnp.float32),
        jnp.zeros(shape_rows + (128,), jnp.float32),
    )
    key_piece = lax.all_gather(key_rows, "ctx", axis=0, tiled=True)
    value_piece = lax.all_gather(value_rows, "ctx", axis=0, tiled=True)
    count = key_piece.shape[0]
    width = math.gcd(count, 512)

    def step(block_index, state):
        offset = block_index * width

        def compute(inner):
            running_max, running_sum, accum = inner
            key_block = lax.dynamic_slice_in_dim(key_piece, block_index * width, width, 0).reshape(
                width, kv_heads, 128
            )
            value_block = lax.dynamic_slice_in_dim(
                value_piece, block_index * width, width, 0
            ).reshape(width, kv_heads, 128)
            scores = (
                jnp.einsum("tkgd,skd->kgts", grouped, key_block, preferred_element_type=jnp.float32)
                * scale
            )
            key_pos = offset + jnp.arange(width, dtype=jnp.int32)
            allowed = key_pos[None, :] <= query_pos[:, None]
            scores = jnp.where(allowed, scores, -jnp.inf)
            new_max = jnp.maximum(running_max, jnp.max(scores, axis=-1))
            factor = jnp.exp(running_max - new_max)
            weights = jnp.exp(scores - new_max[..., None])
            new_sum = running_sum * factor + jnp.sum(weights, axis=-1)
            product = jnp.einsum(
                "kgts,skd->kgtd",
                weights.astype(jnp.bfloat16),
                value_block,
                preferred_element_type=jnp.float32,
            )
            return (new_max, new_sum, accum * factor[..., None] + product)

        return lax.cond(offset <= last_pos, compute, lambda inner: inner, state)

    _, total, accum = lax.fori_loop(0, count // width, step, start_state)
    output = accum / total[..., None]
    return (
        jnp.transpose(output, (2, 0, 1, 3)).reshape(token_count, q_heads * 128).astype(jnp.bfloat16)
    )


def place_rows(expert_ids, sent_rows, capacity, expert_count):
    top_count = expert_ids.shape[1]
    flat_ids = expert_ids.reshape(-1)
    onehot = (flat_ids[:, None] == jnp.arange(expert_count, dtype=jnp.int32)[None, :]).astype(
        jnp.int32
    )
    index = jnp.arange(flat_ids.shape[0], dtype=jnp.int32)
    before = (index[None, :] < index[:, None]).astype(jnp.bfloat16)
    earlier = jnp.dot(
        before, onehot.astype(jnp.bfloat16), preferred_element_type=jnp.float32
    ).astype(jnp.int32)
    slot_index = jnp.sum(earlier * onehot, axis=1)
    destination = flat_ids * capacity + slot_index
    copies = jnp.repeat(sent_rows, top_count, axis=0)
    buffer = (
        jnp.zeros((expert_count * capacity, sent_rows.shape[1]), sent_rows.dtype)
        .at[destination]
        .set(copies)
    )
    return (buffer.reshape(expert_count, 2, capacity // 2, sent_rows.shape[1]), destination)


def per_device(
    queries,
    key_rows,
    value_rows,
    hidden_in,
    out_proj,
    norm_gain,
    expert_ids,
    gate_scores,
    w_gate,
    w_up,
    w_down,
):
    token_count = queries.shape[0]
    model_width = hidden_in.shape[1]
    half_width = model_width // 2
    ctx_size = lax.axis_size("ctx")
    local_experts = w_gate.shape[0]
    expert_count = local_experts * ctx_size
    top_count = expert_ids.shape[1]
    capacity = 2 * (
        min(token_count, max(2, 3 * token_count * top_count // (2 * expert_count))) // 2
    )
    half_cap = capacity // 2
    first = lax.axis_index("ctx") * token_count
    core = lax.axis_index("exp")
    side_start = core * half_width
    attended = attend(queries, key_rows, value_rows, first)
    head_part = jnp.dot(attended, out_proj, preferred_element_type=jnp.float32)
    attn_full = lax.psum(head_part.astype(jnp.bfloat16), "exp").astype(jnp.float32)
    resid = hidden_in.astype(jnp.float32) + attn_full
    inverse = lax.rsqrt(jnp.mean(resid * resid, axis=1, keepdims=True) + 1e-06)
    sent_rows = (resid * inverse * norm_gain[None, :]).astype(jnp.bfloat16)
    resid_half = lax.dynamic_slice_in_dim(resid, side_start, half_width, 1)
    buffer, destination = place_rows(expert_ids, sent_rows, capacity, expert_count)
    own_slots = lax.dynamic_slice_in_dim(buffer, core, 1, 1)
    grouped = lax.all_to_all(own_slots, "ctx", split_axis=0, concat_axis=0, tiled=True)
    gate = jnp.einsum("sxmd,xdf->sxmf", grouped, w_gate, preferred_element_type=jnp.float32)
    upper = jnp.einsum("sxmd,xdf->sxmf", grouped, w_up, preferred_element_type=jnp.float32)
    hidden = (jax.nn.silu(gate) * upper).astype(jnp.bfloat16)
    partial_value = jnp.einsum(
        "sxmf,xfd->sxmd", hidden, w_down, preferred_element_type=jnp.float32
    ).astype(jnp.bfloat16)
    returned = lax.all_to_all(partial_value, "ctx", split_axis=0, concat_axis=0, tiled=True)
    flat_back = returned.reshape(expert_count * half_cap, model_width)
    slot_of = destination % capacity
    expert_of = destination // capacity
    owned = slot_of // half_cap == core
    local_index = jnp.where(owned, expert_of * half_cap + slot_of - core * half_cap, 0)
    picked = flat_back[local_index].astype(jnp.float32)
    mixing = (gate_scores / jnp.sum(gate_scores, axis=1, keepdims=True)).reshape(-1)
    mixing = jnp.where(owned, mixing, 0.0)
    weighted = (picked * mixing[:, None]).reshape(token_count, top_count, model_width)
    mixed_part = jnp.sum(weighted, axis=1)
    moe_half = lax.psum_scatter(
        mixed_part.astype(jnp.bfloat16), "exp", scatter_dimension=1, tiled=True
    ).astype(jnp.float32)
    return (resid_half + moe_half).astype(jnp.bfloat16)


def layer_kernel(
    n,
    q_ref,
    k_ref,
    v_ref,
    hid_ref,
    proj_hbm,
    gain_ref,
    ids_ref,
    gate_ref,
    wg_hbm,
    wu_hbm,
    wd_hbm,
    out_ref,
    kv_buf,
    co_out,
    co_in,
    row_buf,
    con_buf,
    rs_bufs,
    half_out,
    half_in,
    fin_out,
    fin_in,
    queries,
    top,
    den,
    acc,
    att,
    resid,
    by_token,
    proj,
    wg,
    wu,
    wd,
    load_sem,
    kv_sem,
    co_sem,
    w_sem,
    ag_sem,
    rs_sem,
    half_sem,
    fin_sem,
):
    me = lax.axis_index("ctx")
    core = lax.axis_index("exp")
    group = lax.axis_index("groups")
    bits = n.bit_length() - 1
    rows = q_ref.shape[0]
    heads = q_ref.shape[1] // HEAD
    half = rows // 2
    piece_rows = half // PIECES
    width = hid_ref.shape[1]
    side = width // 2
    coord = [(me // 2 ** (bits - 1 - d)) % 2 for d in range(bits)]
    partner = [me + (1 - 2 * coord[d]) * 2 ** (bits - 1 - d) for d in range(bits)]
    far, near, last = list(range(bits - 2)), bits - 2, bits - 1
    kv_orders = [
        far + [near, last],
        far + [last, near],
        [near, last] + far,
        [last] + far + [near],
    ]
    orders = [far + [near], far + [near], far + [near], [near] + far]
    places = n // 2
    parity = coord[last]
    other = 1 - core

    halves = [pl.ds(pl.multiple_of(core * (w.shape[1] // 2), 16), w.shape[1] // 2) for w in (wg, wu, wd)]
    loads = [
        pltpu.make_async_copy(src, dst, load_sem.at[i])
        for i, (src, dst) in enumerate(
            [
                (proj_hbm, proj),
                (wg_hbm.at[0], wg.at[parity]),
                (wu_hbm.at[0], wu.at[parity]),
                (wd_hbm.at[0], wd.at[parity]),
            ]
        )
    ]
    for load in loads:
        load.start()

    barrier = pltpu.get_barrier_semaphore()
    for hop in range(1, n):
        pl.semaphore_signal(
            barrier, inc=1, device_id=(group, (me + hop) % n, core), device_id_type=MESH
        )
    pl.semaphore_signal(barrier, inc=1, device_id=(group, me, other), device_id_type=MESH)

    own = tuple(coord)
    for i, ref in enumerate((k_ref, v_ref)):
        kv_buf[(2 * i,) + own] = ref[:half, :]
        kv_buf[(2 * i + 1,) + own] = ref[half:, :]
    mix = gate_ref[...] / jnp.sum(gate_ref[...], axis=1, keepdims=True)
    lane = lax.broadcasted_iota(jnp.int32, (rows, HEAD), 1)
    coef = jnp.zeros((rows, HEAD), jnp.float32)
    for k in range(ids_ref.shape[1]):
        coef = coef + jnp.where(ids_ref[:, k : k + 1] == lane, mix[:, k : k + 1], 0.0)
    by_expert = coef.T
    co_out[...] = jnp.zeros(co_out.shape, jnp.float32)
    for e in range(places):
        co_out[e, :2, :] = by_expert[2 * e : 2 * e + 2, :]
    pl.semaphore_wait(barrier, n)

    def expert_copy(i):
        return pltpu.make_async_remote_copy(
            src_ref=(wg_hbm, wu_hbm, wd_hbm)[i].at[0, halves[i]],
            dst_ref=(wg, wu, wd)[i].at[parity, halves[i]],
            send_sem=w_sem.at[i, 0, 0],
            recv_sem=w_sem.at[i, 0, 1],
            device_id=(group, partner[last], core),
            device_id_type=MESH,
        )

    def share_copy(i):
        here = (wg, wu, wd)[i].at[1 - parity, halves[i]]
        return pltpu.make_async_remote_copy(
            src_ref=here,
            dst_ref=here,
            send_sem=w_sem.at[i, 1, 0],
            recv_sem=w_sem.at[i, 1, 1],
            device_id=(group, me, other),
            device_id_type=MESH,
        )

    def share(i):
        copy = expert_copy(i)
        copy.wait_recv()
        share_copy(i).start()
        sent.extend([copy, share_copy(i)])

    def weight_copy(hop):
        to = (me + 2 * hop) % n
        return pltpu.make_async_remote_copy(
            src_ref=co_out.at[to // 2],
            dst_ref=co_in.at[me // 2],
            send_sem=co_sem.at[hop, 0],
            recv_sem=co_sem.at[hop, 1],
            device_id=(group, to, core),
            device_id_type=MESH,
        )

    def gather(buf, lead, order, step, sems):
        done = order[:step]
        where = lead + tuple(
            slice(None) if d in done else coord[d] for d in range(len(order))
        )
        return pltpu.make_async_remote_copy(
            src_ref=buf.at[where],
            dst_ref=buf.at[where],
            send_sem=sems[0],
            recv_sem=sems[1],
            device_id=(group, partner[order[step]], core),
            device_id_type=MESH,
        )

    sent = []

    def kv_copy(i, step):
        return gather(
            kv_buf, (i,), kv_orders[i], step, (kv_sem.at[i, step, 0], kv_sem.at[i, step, 1])
        )

    for i in range(4):
        kv_copy(i, 0).start()
    for hop in range(1, places):
        copy = weight_copy(hop)
        copy.start()
        sent.append(copy)
    for h in range(heads):
        queries[h] = q_ref[:, h * HEAD : (h + 1) * HEAD]
    top[...] = jnp.full(top.shape, NEG, jnp.float32)
    den[...] = jnp.zeros(den.shape, jnp.float32)
    acc[...] = jnp.zeros(acc.shape, jnp.float32)
    for step in range(bits):
        for i in range(4):
            copy = kv_copy(i, step)
            copy.wait_recv()
            sent.append(copy)
            if step < bits - 1:
                kv_copy(i, step + 1).start()

    for i in range(3):
        expert_copy(i).start()

    span = 4 * rows
    chunk = me // 4
    unit = HEAD ** (-0.5) * math.log2(math.e)
    row_pos = lax.broadcasted_iota(jnp.int32, (rows, span), 0) + (me % 4) * rows
    column = lax.broadcasted_iota(jnp.int32, (rows, span), 1)
    col_pos = (column % (2 * rows)) // half * rows + column // (2 * rows) * half + column % half

    def attend_chunk(j, carry):
        at = tuple((j // 2 ** (bits - 3 - d)) % 2 for d in range(bits - 2))
        keys, values = (
            jnp.concatenate(
                [kv_buf[(i,) + at].reshape(2 * rows, HEAD) for i in pair], axis=0
            )
            for pair in ((0, 1), (2, 3))
        )
        allowed = col_pos <= row_pos + (chunk - j) * span
        for h in range(heads):
            scores = lax.dot_general(
                queries[h], keys, (((1,), (1,)), ((), ())), preferred_element_type=jnp.float32
            )
            scores = jnp.where(allowed, scores, NEG)
            old = top[h][:, :1]
            new = jnp.maximum(old, jnp.max(scores, axis=1, keepdims=True))
            factor = jnp.exp2((old - new) * unit)
            weights = jnp.exp2((scores - new) * unit)
            total = den[h][:, :1] * factor + jnp.sum(weights, axis=1, keepdims=True)
            product = jnp.dot(
                weights.astype(jnp.bfloat16), values, preferred_element_type=jnp.float32
            )
            acc[h] = acc[h] * factor + product
            top[h] = jnp.broadcast_to(new, (rows, HEAD))
            den[h] = jnp.broadcast_to(total, (rows, HEAD))
        return carry

    lax.fori_loop(0, chunk + 1, attend_chunk, 0)
    for h in range(heads):
        att[:, h * HEAD : (h + 1) * HEAD] = (acc[h] / den[h]).astype(jnp.bfloat16)

    loads[0].wait()
    mine = pl.ds(pl.multiple_of(core * half, half), half)
    theirs = pl.ds(pl.multiple_of(other * half, half), half)
    half_out[...] = jnp.dot(
        att[theirs, :], proj[...], preferred_element_type=jnp.float32
    ).astype(jnp.bfloat16)
    swap = pltpu.make_async_remote_copy(
        src_ref=half_out,
        dst_ref=half_in,
        send_sem=half_sem.at[0],
        recv_sem=half_sem.at[1],
        device_id=(group, me, other),
        device_id_type=MESH,
    )
    swap.start()
    resid[...] = hid_ref[mine, :].astype(jnp.float32) + jnp.dot(
        att[mine, :], proj[...], preferred_element_type=jnp.float32
    )
    by_token[...] = jnp.zeros(by_token.shape, jnp.float32)
    co_in[me // 2] = co_out[me // 2]
    for hop in range(1, places):
        weight_copy(hop).wait_recv()
    for b in range(places):
        for j in range(2):
            by_token[j * places + b : j * places + b + 1, :] = co_in[b, j : j + 1, :]
    by_token[...] = by_token[...].T
    swap.wait_recv()
    sent.append(swap)
    full = resid[...] + half_in[...].astype(jnp.float32)
    resid[...] = full
    inverse = lax.rsqrt(jnp.mean(full * full, axis=1, keepdims=True) + 1e-06)
    normed = (full * inverse * gain_ref[...]).astype(jnp.bfloat16)

    def row_copy(p, step):
        return gather(
            row_buf, (p,), orders[p], step, (ag_sem.at[p, step, 0], ag_sem.at[p, step, 1])
        )

    def rs_copy(p, step):
        order = orders[p][::-1]
        done = order[:step]
        turn = order[step]
        where = (p,) + tuple(
            coord[d] if d in done else (1 - coord[d] if d == turn else slice(None))
            for d in range(bits - 1)
        )
        return pltpu.make_async_remote_copy(
            src_ref=con_buf.at[where],
            dst_ref=rs_bufs[step].at[p],
            send_sem=rs_sem.at[p, step, 0],
            recv_sem=rs_sem.at[p, step, 1],
            device_id=(group, partner[turn], core),
            device_id_type=MESH,
        )

    def fin_copy(p):
        return pltpu.make_async_remote_copy(
            src_ref=fin_out.at[p],
            dst_ref=fin_in.at[p],
            send_sem=fin_sem.at[p, 0],
            recv_sem=fin_sem.at[p, 1],
            device_id=(group, me, other),
            device_id_type=MESH,
        )

    def experts(p):
        if p == 0:
            share(2)
            for load in loads[1:]:
                load.wait()
            for i in range(3):
                share_copy(i).wait_recv()
        x = row_buf[p].reshape(places * piece_rows, width)
        first = pl.multiple_of(core * half + p * piece_rows, piece_rows)
        columns = by_token[pl.ds(first, piece_rows), :]
        parts = []
        for j in range(2):
            gate = jnp.dot(x, wg[j], preferred_element_type=jnp.float32)
            upper = jnp.dot(x, wu[j], preferred_element_type=jnp.float32)
            hidden = (gate / (1.0 + jnp.exp(-gate)) * upper).astype(jnp.bfloat16)
            parts.append(jnp.dot(hidden, wd[j], preferred_element_type=jnp.float32))
        for b in range(places):
            at = tuple((b // 2 ** (bits - 2 - d)) % 2 for d in range(bits - 1))
            some = slice(b * piece_rows, (b + 1) * piece_rows)
            con_buf[(p,) + at] = (
                parts[0][some] * columns[:, b : b + 1]
                + parts[1][some] * columns[:, places + b : places + b + 1]
            ).astype(jnp.bfloat16)

    def stage(p, s):
        if s == 0:
            row_buf[(p,) + own[:-1]] = normed[p * piece_rows : (p + 1) * piece_rows]
            row_copy(p, 0).start()
            return
        if s < bits:
            copy = row_copy(p, s - 1)
            copy.wait_recv()
            sent.append(copy)
            if s < bits - 1:
                row_copy(p, s).start()
                return
            experts(p)
            rs_copy(p, 0).start()
            return
        s -= bits
        if s < bits - 1:
            copy = rs_copy(p, s)
            copy.wait_recv()
            sent.append(copy)
            order = orders[p][::-1]
            where = (p,) + tuple(
                coord[d] if d in order[: s + 1] else slice(None) for d in range(bits - 1)
            )
            total = con_buf[where].astype(jnp.float32) + rs_bufs[s][p].astype(jnp.float32)
            if s < bits - 2:
                con_buf[where] = total.astype(jnp.bfloat16)
                rs_copy(p, s + 1).start()
                return
            result = resid[p * piece_rows : (p + 1) * piece_rows] + total
            result = result.astype(jnp.bfloat16)
            left, right = result[:, :side], result[:, side:]
            fin_out[p] = jnp.where(core == 0, right, left)
            fin_copy(p).start()
            first = pl.multiple_of(core * half + p * piece_rows, piece_rows)
            out_ref[pl.ds(first, piece_rows), :] = jnp.where(core == 0, left, right)
            return
        copy = fin_copy(p)
        copy.wait_recv()
        sent.append(copy)
        first = pl.multiple_of(other * half + p * piece_rows, piece_rows)
        out_ref[pl.ds(first, piece_rows), :] = fin_in[p]

    stages = 2 * bits
    plan = sorted((s + STAGGER * p, p, s) for p in range(PIECES) for s in range(stages))
    for _, p, s in plan:
        if p == 0 and 1 <= s < 3:
            share(s - 1)
        stage(p, s)
    for copy in sent:
        copy.wait_send()


def fused_layer(n, *args):
    queries, key_rows, value_rows, hidden_in, out_proj = args[:5]
    norm_gain, expert_ids, gate_scores, w_gate, w_up, w_down = args[5:]
    rows, width = hidden_in.shape
    heads = queries.shape[1] // HEAD
    bits = n.bit_length() - 1
    half = rows // 2
    piece_rows = half // PIECES
    cube = (2,) * bits
    vmem = pl.BlockSpec(memory_space=pltpu.VMEM)
    anywhere = pl.BlockSpec(memory_space=pl.ANY)
    bf16, f32 = jnp.bfloat16, jnp.float32
    scratch = [
        pltpu.VMEM((4,) + cube + (half, HEAD), bf16),
        pltpu.VMEM((n // 2, 8, rows), f32),
        pltpu.VMEM((n // 2, 8, rows), f32),
        pltpu.VMEM((PIECES,) + cube[1:] + (piece_rows, width), bf16),
        pltpu.VMEM((PIECES,) + cube[1:] + (piece_rows, width), bf16),
        [
            pltpu.VMEM((PIECES,) + cube[s + 2 :] + (piece_rows, width), bf16)
            for s in range(bits - 1)
        ],
        pltpu.VMEM((half, width), bf16),
        pltpu.VMEM((half, width), bf16),
        pltpu.VMEM((PIECES, piece_rows, width // 2), bf16),
        pltpu.VMEM((PIECES, piece_rows, width // 2), bf16),
        pltpu.VMEM((heads, rows, HEAD), bf16),
        pltpu.VMEM((heads, rows, HEAD), f32),
        pltpu.VMEM((heads, rows, HEAD), f32),
        pltpu.VMEM((heads, rows, HEAD), f32),
        pltpu.VMEM((rows, heads * HEAD), bf16),
        pltpu.VMEM((half, width), f32),
        pltpu.VMEM((rows, rows), f32),
        pltpu.VMEM(out_proj.shape, bf16),
        pltpu.VMEM((2,) + w_gate.shape[1:], bf16),
        pltpu.VMEM((2,) + w_up.shape[1:], bf16),
        pltpu.VMEM((2,) + w_down.shape[1:], bf16),
        pltpu.SemaphoreType.DMA((4,)),
        pltpu.SemaphoreType.DMA((4, bits, 2)),
        pltpu.SemaphoreType.DMA((n, 2)),
        pltpu.SemaphoreType.DMA((3, 2, 2)),
        pltpu.SemaphoreType.DMA((PIECES, bits - 1, 2)),
        pltpu.SemaphoreType.DMA((PIECES, bits - 1, 2)),
        pltpu.SemaphoreType.DMA((2,)),
        pltpu.SemaphoreType.DMA((PIECES, 2)),
    ]
    return pl.pallas_call(
        functools.partial(layer_kernel, n),
        out_shape=jax.ShapeDtypeStruct((rows, width // 2), bf16),
        in_specs=[vmem] * 4 + [anywhere] + [vmem] * 3 + [anywhere] * 3,
        out_specs=vmem,
        scratch_shapes=scratch,
        compiler_params=pltpu.CompilerParams(
            collective_id=0, has_side_effects=True, vmem_limit_bytes=48 * 2**20
        ),
    )(
        queries,
        key_rows,
        value_rows,
        hidden_in,
        out_proj,
        norm_gain.reshape(1, width),
        expert_ids,
        gate_scores,
        w_gate,
        w_up,
        w_down,
    )


def fits_fused(n, cores, args):
    queries, key_rows, hidden_in = args[0], args[1], args[3]
    expert_ids, w_gate, w_down = args[6], args[8], args[10]
    rows, width = hidden_in.shape
    return (
        cores == 2
        and n >= 8
        and n & (n - 1) == 0
        and n <= HEAD
        and w_gate.shape[0] == 1
        and w_gate.shape[1] % 32 == 0
        and w_down.shape[1] % 32 == 0
        and 2 * expert_ids.shape[1] >= n
        and key_rows.shape[1] == HEAD
        and rows == HEAD
        and width % (2 * HEAD) == 0
        and n * rows * width * 2 <= 8 * 2**20
    )


def layer(*args):
    n, cores = lax.axis_size("ctx"), lax.axis_size("exp")
    if fits_fused(n, cores, args):
        return fused_layer(n, *args)
    return per_device(*args)


def solution(mesh):
    placed = (
        P(("groups", "ctx"), "exp"),
        P(("groups", "ctx"), "exp"),
        P(("groups", "ctx"), "exp"),
        P(("groups", "ctx"), None),
        P("exp", None),
        P(),
        P(("groups", "ctx"), None),
        P(("groups", "ctx"), None),
        P("ctx", None, None),
        P("ctx", None, None),
        P("ctx", None, None),
    )
    return jax.shard_map(
        layer,
        mesh=mesh,
        in_specs=placed,
        out_specs=P(("groups", "ctx"), "exp"),
        check_vma=False,
    )
```
